256 devices in a mesh: dp: 64 (over z_lo, y, x), mp: 4 (over z_hi, core).
Axes of the slice: x: 4, y: 4, z: 8 (z_hi: 2, z_lo: 4; z = z_hi * 4 + z_lo), core: 2. Of those that a mesh axis runs over, the one named last changes fastest.
Arguments:
- frames: bfloat16 [256, 256, 256], P('dp', 'mp'), may hold values from -6 to 6
- frame_offsets: int32 [256], P('dp'), may hold values from -1 to 3, as said below
- first_weight: bfloat16 [27, 256, 256], P(None, 'mp'), may hold values from -0.078125 to 0.078125
- second_weight: bfloat16 [27, 256, 256], P(None, 'mp'), may hold values from -0.078125 to 0.078125
- cotangent: bfloat16 [256, 256, 256], P('dp', 'mp'), may hold values from -0.125 to 0.125
Outputs:
- output: bfloat16 [256, 256, 256], P('dp', 'mp')
- first_grad: float32 [27, 256, 256], P(None, 'mp', 'dp')
- second_grad: float32 [27, 256, 256], P(None, 'mp', 'dp')
The draws below stay inside these ranges and needn't reach their ends.
Inputs may be any that keep to these rules, and one draw needn't show every extreme that they name: `frame_offsets`: on each index of dp the live slots come first and the empty ones (-1) after; a clip's frames stand in consecutive slots of one index of dp, numbered 0, 1, 2 and so on; every index of dp has a live slot, and some index holds one clip of 4 frames.
All inputs are finite; a program needn't handle non-finite values.
Results may differ from the reference program's by a relative error of at most 0.003.
Values may be sent and summed in bfloat16 or wider, within the bound.
No kernel may reach another device: no remote copies, remote signals or barrier semaphores. Data moves between devices by JAX's collectives and lax.ppermute only.
A program may use at most 64 MiB of HBM per device.

```python
import jax
import jax.numpy as jnp
from jax import lax

C = 256
TAPS = 27
SIDE = 16
FR_DEV = 4
PIXELS = 256
SLOTS = 256


def draw_frame_offsets(key, part):
    key = jax.random.fold_in(key, 11)
    key_live, key_full, key_start = jax.random.split(key, 3)
    shards = SLOTS // FR_DEV
    live_count = jax.random.randint(key_live, (shards,), 1, FR_DEV + 1)
    full_shard = jax.random.randint(key_full, (), 0, shards)
    position = jnp.arange(FR_DEV, dtype=jnp.int32)
    shard_ids = jnp.arange(shards, dtype=jnp.int32)
    starts = jax.random.randint(key_start, (shards, FR_DEV), 0, 4) == 0
    starts = starts | (position == 0)[None, :]
    starts = jnp.where((shard_ids == full_shard)[:, None], (position == 0)[None, :], starts)
    live_count = jnp.where(shard_ids == full_shard, FR_DEV, live_count)
    last_start = lax.cummax(jnp.where(starts, position[None, :], 0), axis=1)
    offsets = position[None, :] - last_start
    offsets = jnp.where(position[None, :] < live_count[:, None], offsets, -1)
    return offsets.reshape(-1).astype(jnp.int32)


def block_scale(own_key, dims, cuts, smallest, largest):
    loudness = 1.0
    for axis_at, blocks in cuts:
        steps = jax.random.uniform(jax.random.fold_in(jax.random.fold_in(own_key, 6), axis_at), (blocks,), jnp.float32, smallest / len(cuts), largest / len(cuts))
        loudness = loudness * jnp.repeat(jnp.exp(steps), dims[axis_at] // blocks).reshape((-1,) + (1,) * (len(dims) - 1 - axis_at))
    return loudness


def scatter_about(stream_key, extent, spread, limit, cuts=(), kind=jnp.bfloat16):
    drawn = jax.random.normal(stream_key, extent, jnp.float32) * spread
    if len(cuts) > 0:
        drawn = block_scale(stream_key, extent, cuts, -0.22, 0.18) * drawn
    return jnp.clip(drawn, min=-limit, max=limit).astype(kind)


def setup_inputs(seed: int = 0) -> dict:
    seeds = jax.random.split(jax.random.key(seed), 6)
    frames = scatter_about(seeds[0], (SLOTS, C, PIXELS), 1.0, 6.0, ((0, 64), (1, 4)))
    frame_offsets = draw_frame_offsets(jax.random.fold_in(seeds[5], 71), 0)
    first_weight = scatter_about(seeds[2], (TAPS, C, C), (TAPS * C) ** -0.5, 0.078125, ((1, 4),))
    second_weight = scatter_about(seeds[3], (TAPS, C, C), (TAPS * C) ** -0.5, 0.078125, ((1, 4),))
    cotangent = scatter_about(seeds[4], (SLOTS, C, PIXELS), (2.0 / (SLOTS * PIXELS) ** 0.5), 0.125, ((0, 64), (1, 4)))
    return dict(frames=frames, frame_offsets=frame_offsets, first_weight=first_weight, second_weight=second_weight, cotangent=cotangent)


def shift_flat(values, step, tile_side):
    pixels = tile_side * tile_side
    padded = jnp.pad(values, ((0, 0), (0, 0), (tile_side + 1, tile_side + 1)))
    return padded[:, :, tile_side + 1 + step:tile_side + 1 + step + pixels]

def tap_mask(row_step, col_step, tile_side, dtype):
    position = jnp.arange(tile_side * tile_side, dtype=jnp.int32)
    pixel_row = position // tile_side
    pixel_col = position % tile_side
    inside = (pixel_row + row_step >= 0) & (pixel_row + row_step < tile_side)
    inside = inside & (pixel_col + col_step >= 0) & (pixel_col + col_step < tile_side)
    return inside.astype(dtype)

def source_rows(offsets, frame_lag):
    indices = jnp.arange(offsets.shape[0], dtype=jnp.int32)
    return (indices - jnp.minimum(jnp.maximum(offsets, 0), frame_lag)).astype(jnp.int32)

def conv_forward(source, weight, offsets, tile_side):
    result = jnp.zeros((source.shape[0], weight.shape[1], source.shape[2]), jnp.float32)
    for frame_lag in range(3):
        earlier = jnp.take(source, source_rows(offsets, frame_lag), axis=0)
        for row_step in (-1, 0, 1):
            for col_step in (-1, 0, 1):
                tap_index = frame_lag * 9 + (row_step + 1) * 3 + (col_step + 1)
                shifted = shift_flat(earlier, row_step * tile_side + col_step, tile_side)
                shifted = shifted * tap_mask(row_step, col_step, tile_side, source.dtype)
                result = result + jnp.einsum('oi,fip->fop', weight[tap_index].astype(jnp.float32), shifted.astype(jnp.float32))
    return result

def weight_grad(cotangent, source, offsets, tile_side):
    pieces = []
    for frame_lag in range(3):
        earlier = jnp.take(source, source_rows(offsets, frame_lag), axis=0)
        for row_step in (-1, 0, 1):
            for col_step in (-1, 0, 1):
                shifted = shift_flat(earlier, row_step * tile_side + col_step, tile_side)
                shifted = shifted * tap_mask(row_step, col_step, tile_side, source.dtype)
                pieces.append(jnp.einsum('fop,fip->oi', cotangent.astype(jnp.float32), shifted.astype(jnp.float32)))
    return jnp.stack(pieces)

def conv_adjoint(cotangent, weight, offsets, tile_side):
    result = jnp.zeros((cotangent.shape[0], weight.shape[2], cotangent.shape[2]), jnp.float32)
    for frame_lag in range(3):
        lag_sum = jnp.zeros_like(result)
        for row_step in (-1, 0, 1):
            for col_step in (-1, 0, 1):
                tap_index = frame_lag * 9 + (row_step + 1) * 3 + (col_step + 1)
                product_term = jnp.einsum('oi,fop->fip', weight[tap_index].astype(jnp.float32), cotangent.astype(jnp.float32))
                product_term = product_term * tap_mask(row_step, col_step, tile_side, jnp.float32)
                lag_sum = lag_sum + shift_flat(product_term, -(row_step * tile_side + col_step), tile_side)
        result = result.at[source_rows(offsets, frame_lag)].add(lag_sum)
    return result

def reference(frames, frame_offsets, first_weight, second_weight, cotangent):
    tile_side = SIDE
    pre_act = conv_forward(frames, first_weight, frame_offsets, tile_side)
    hidden = jax.nn.silu(pre_act).astype(jnp.bfloat16)
    output = (frames.astype(jnp.float32) + conv_forward(hidden, second_weight, frame_offsets, tile_side)).astype(jnp.bfloat16)
    live_mask = (frame_offsets >= 0).astype(jnp.bfloat16)
    masked = cotangent * live_mask[:, None, None]
    second_grad = weight_grad(masked, hidden, frame_offsets, tile_side)
    hidden_grad = conv_adjoint(masked, second_weight, frame_offsets, tile_side)
    sigma_value = jax.nn.sigmoid(pre_act)
    pre_grad = (hidden_grad * sigma_value * (1.0 + pre_act * (1.0 - sigma_value))).astype(jnp.bfloat16)
    first_grad = weight_grad(pre_grad, frames, frame_offsets, tile_side)
    return (output, first_grad, second_grad)
```

```python
import functools

import jax
import jax.numpy as jnp
from jax import lax
from jax.experimental import pallas as pl
from jax.experimental.pallas import tpu as pltpu
from jax.sharding import PartitionSpec as P

F32, BF16 = jnp.float32, jnp.bfloat16
SIDE, PIX, FR, CH, OWN, TAPS = 16, 256, 4, 256, 64, 27
STEPS = tuple((u, v) for u in (-1, 0, 1) for v in (-1, 0, 1))
LANES = 1792
PIECE = 112
XY_GROUPS = [[z * 16 + r for r in range(16)] for z in range(4)]


def place(zl, y, x):
    return (zl * 4 + y) * 4 + x


def dp_perm(move):
    return [
        (place(z, y, x), place(*move(z, y, x)))
        for z in range(4) for y in range(4) for x in range(4)
    ]


def all_perm(move):
    pairs = []
    for z in range(4):
        for y in range(4):
            for x in range(4):
                for m in range(4):
                    z2, y2, x2, m2 = move(z, y, x, m)
                    pairs.append((place(z, y, x) * 4 + m, place(z2, y2, x2) * 4 + m2))
    return pairs


def mp_perm(flip):
    return [(m, m ^ flip) for m in range(4)]


def call(kernel, outs, scratch, args, flops=0, smem=1):
    specs = [pl.BlockSpec(memory_space=pltpu.SMEM)] * smem
    specs += [pl.BlockSpec(memory_space=pltpu.VMEM)] * (len(args) - smem)
    size = sum(a.size * a.dtype.itemsize for a in args)
    return pl.pallas_call(
        kernel,
        out_shape=outs,
        in_specs=specs,
        out_specs=jax.tree.map(lambda _: pl.BlockSpec(memory_space=pltpu.VMEM), outs),
        scratch_shapes=scratch,
        cost_estimate=pl.CostEstimate(flops=flops, bytes_accessed=size, transcendentals=0),
        compiler_params=pltpu.CompilerParams(vmem_limit_bytes=48 * 2**20),
    )(*args)


def shape(dims, kind):
    return jax.ShapeDtypeStruct(dims, kind)


def inside(u, v):
    pos = lax.broadcasted_iota(jnp.int32, (1, PIX), 1)
    row, col = pos >> 4, pos & 15
    ok = (row + u >= 0) & (row + u < SIDE) & (col + v >= 0) & (col + v < SIDE)
    return jnp.where(ok, 1.0, 0.0).astype(F32)


def turn(value, step):
    return value if step % PIX == 0 else pltpu.roll(value, step % PIX, 1)


def source(meta, f, lag):
    return f - jnp.minimum(jnp.maximum(meta[f], 0), lag)


def nt(a, b):
    return lax.dot_general(a, b, (((1,), (1,)), ((), ())), preferred_element_type=F32)


def nn(a, b):
    return lax.dot_general(a, b, (((1,), (0,)), ((), ())), preferred_element_type=F32)


def rows(start, size):
    return pl.ds(pl.multiple_of(start, size), size)


def gather_rows(meta, pieces, out, live=False):
    m = meta[7]
    for f in range(FR):
        for flip, piece in enumerate(pieces):
            value = piece[f]
            if live:
                value = (value.astype(F32) * jnp.where(meta[f] >= 0, 1.0, 0.0)).astype(BF16)
            out[f, rows((m ^ flip) * OWN, OWN), :] = value


def conv_into(meta, weight, maps, prod, finish):
    def product(s, _):
        for lag in range(3):
            w = weight[9 * lag:9 * lag + 9].reshape(9 * OWN, CH)
            prod[s, lag] = nn(w, maps[s])
        return 0
    lax.fori_loop(0, FR, product, 0)

    def collect(f, _):
        src = [source(meta, f, lag) for lag in range(3)]
        total = jnp.zeros((OWN, PIX), F32)
        for i, (u, v) in enumerate(STEPS):
            part = slice(i * OWN, (i + 1) * OWN)
            value = prod[src[0], 0, part, :] + prod[src[1], 1, part, :] + prod[src[2], 2, part, :]
            total = total + turn(value, -(SIDE * u + v)) * inside(u, v)
        finish(f, total)
        return 0
    lax.fori_loop(0, FR, collect, 0)


def first_conv(meta, f0, f1, f2, f3, weight, pre, hidden, ordered, maps, prod):
    gather_rows(meta, (f0, f1, f2, f3), maps)

    def finish(f, total):
        pre[f] = total
        hidden[f] = (total / (1.0 + jnp.exp(-total))).astype(BF16)
    conv_into(meta, weight, maps, prod, finish)
    r = lax.broadcasted_iota(jnp.int32, (CH, CH), 0)
    c = lax.broadcasted_iota(jnp.int32, (CH, CH), 1)
    want = ((r >> 2) & 3) * 64 + ((r >> 4) & 3) * 16 + (r >> 6) * 4 + (r & 3)
    pick = jnp.where(c == want, 1.0, 0.0).astype(BF16)
    for f in range(FR):
        ordered[f] = nn(pick, maps[f]).astype(BF16)


def second_conv(meta, h0, h1, h2, h3, weight, frames, out, maps, prod):
    gather_rows(meta, (h0, h1, h2, h3), maps)

    def finish(f, total):
        out[f] = (frames[f].astype(F32) + total).astype(BF16)
    conv_into(meta, weight, maps, prod, finish)


def second_grad_part(meta, c0, c1, c2, c3, hidden, s1, s2, s3, own, maps, taps, total):
    gather_rows(meta, (c0, c1, c2, c3), maps, live=True)
    for f in range(FR):
        h = hidden[f].astype(F32)
        for i, (u, v) in enumerate(STEPS):
            taps[f, i * OWN:(i + 1) * OWN, :] = (turn(h, -(SIDE * u + v)) * inside(u, v)).astype(BF16)
    cot = jnp.concatenate([maps[f] for f in range(FR)], axis=1)
    for lag in range(3):
        lhs = jnp.concatenate([taps[source(meta, f, lag)] for f in range(FR)], axis=1)
        total[9 * lag:9 * lag + 9] = nt(lhs, cot).reshape(9, OWN, CH)
    y = meta[5]
    own[...] = total[:, rows(y * 16, 16), :]
    for r, out in ((1, s1), (2, s2), (3, s3)):
        out[...] = total[:, rows(((y + r) & 3) * 16, 16), :].astype(BF16)


def hidden_grad_part(meta, c_own, c_z, w_own, w_z, keep, send, taps, flipped, total):
    zh, core = meta[7] >> 1, meta[7] & 1
    eye = jnp.where(
        lax.broadcasted_iota(jnp.int32, (128, 128), 0) == lax.broadcasted_iota(jnp.int32, (128, 128), 1),
        1.0, 0.0,
    ).astype(BF16)
    half = rows(zh * 128, 128)
    for lag in range(3):
        w = w_own[9 * lag:9 * lag + 9, :, half].reshape(9 * OWN, 128)
        flipped[0, lag] = nt(eye, w).astype(BF16)
        lo, hi = 9 * OWN * lag, 9 * OWN * (lag + 1)
        if lag < 2:
            w = w_z[lo:hi]
        else:
            w = jnp.concatenate([w_z[lo:1680], w_z[1680 + 64:hi + 64]], axis=0)
        flipped[1, lag] = nt(eye, w).astype(BF16)
    total[...] = jnp.zeros(total.shape, F32)

    def slot(f, _):
        live = jnp.where(meta[f] >= 0, 1.0, 0.0)
        for who, ref in ((0, c_own), (1, c_z)):
            g = ref[f].astype(F32) * live
            for i, (u, v) in enumerate(STEPS):
                taps[who, i * OWN:(i + 1) * OWN, :] = turn(g * inside(u, v), SIDE * u + v).astype(BF16)
        for lag in range(3):
            at = source(meta, f, lag)
            total[at] = total[at] + nn(flipped[0, lag], taps[0]) + nn(flipped[1, lag], taps[1])
        return 0
    lax.fori_loop(0, FR, slot, 0)
    keep[...] = total[:, rows(core * OWN, OWN), :]
    send[...] = total[:, rows((1 - core) * OWN, OWN), :]


def first_grad_part(meta, pre, ha, hb, ordered, s1, s2, s3, own, taps, total):
    for f in range(FR):
        p = pre[f]
        sigma = 1.0 / (1.0 + jnp.exp(-p))
        g = ((ha[f] + hb[f]) * sigma * (1.0 + p * (1.0 - sigma))).astype(BF16).astype(F32)
        for i, (u, v) in enumerate(STEPS):
            taps[i * OWN:(i + 1) * OWN, f * PIX:(f + 1) * PIX] = turn(g * inside(u, v), SIDE * u + v).astype(BF16)
    for lag in range(3):
        lhs = jnp.concatenate([ordered[source(meta, f, lag)] for f in range(FR)], axis=1)
        total[:, 576 * lag:576 * lag + 576] = nt(lhs, taps[...])
    total[:, 1728:LANES] = jnp.zeros((CH, LANES - 1728), F32)
    x = meta[6]
    own[...] = total[rows(x * 64, 64), :]
    for r, out in ((1, s1), (2, s2), (3, s3)):
        out[...] = total[rows(((x + r) & 3) * 64, 64), :].astype(BF16)


def first_grad_y(meta, own, r1, r2, r3, s1, s2, s3, keep, total):
    total[...] = own[...] + r1[...].astype(F32) + r2[...].astype(F32) + r3[...].astype(F32)
    y = meta[5]
    keep[...] = total[rows(y * 16, 16), :]
    for r, out in ((1, s1), (2, s2), (3, s3)):
        out[...] = total[rows(((y + r) & 3) * 16, 16), :].astype(BF16)


def first_grad_z(meta, own, r1, r2, r3, keep, s1, s2, s3):
    total = own[...] + r1[...].astype(F32) + r2[...].astype(F32) + r3[...].astype(F32)
    for r, out in ((0, keep), (1, s1), (2, s2), (3, s3)):
        z = (meta[4] + r) & 3
        value = total[0:4]
        for j in range(1, 4):
            value = jnp.where(z == j, total[4 * j:4 * j + 4], value)
        out[...] = value


def second_grad_x(meta, own, r1, r2, r3, s1, s2, s3, keep, total):
    for h in range(2):
        lane = slice(128 * h, 128 * h + 128)
        value = own[:, :, lane] + r1[:, :, lane].astype(F32) + r2[:, :, lane].astype(F32) + r3[:, :, lane].astype(F32)
        total[h, 0:432, :] = value.reshape(432, 128)
        total[h, 432:512, :] = jnp.zeros((80, 128), F32)
    for r, out in ((0, keep), (1, s1), (2, s2), (3, s3)):
        x = (meta[6] + r) & 3
        for i in range(4):
            for h in range(2):
                value = total[h, pl.ds(x * 4 + i, 32, stride=16), :]
                out[i, :, 128 * h:128 * h + 128] = value.astype(out.dtype)


def second_grad_z(meta, own, r1, r2, r3, p0, p1, p2, p3, total):
    for h in range(2):
        lane = slice(128 * h, 128 * h + 128)
        total[h] = own[:, :, lane] + r1[:, :, lane].astype(F32) + r2[:, :, lane].astype(F32) + r3[:, :, lane].astype(F32)
    low = lax.broadcasted_iota(jnp.int32, (32, 128), 1) < 64
    for r, out in enumerate((p0, p1, p2, p3)):
        q = meta[4] ^ r
        even = (q & 1) == 0
        for j in range(2):
            a, b = total[q >> 1, j], total[q >> 1, j + 2]
            a2, b2 = pltpu.roll(a, 64, 1), pltpu.roll(b, 64, 1)
            out[j] = jnp.where(low, jnp.where(even, a, a2), jnp.where(even, b2, b))


def local(frames, frame_offsets, first_weight, second_weight, cotangent):
    d, m = lax.axis_index("dp"), lax.axis_index("mp")
    zl, y, x = d // 16, (d // 4) % 4, d % 4
    meta = jnp.concatenate([frame_offsets, jnp.stack([zl, y, x, m]).astype(jnp.int32)])

    start = jnp.minimum(PIECE * (d % 16), TAPS * OWN - PIECE)
    piece = lax.dynamic_slice(second_weight.reshape(TAPS * OWN, CH), (start, (1 - m // 2) * 128), (PIECE, 128))
    piece = lax.ppermute(piece, ("dp", "mp"), all_perm(lambda z, y, x, m: (3 - z, y, x, m ^ 2)))
    f_z = lax.ppermute(frames, "mp", mp_perm(2))
    c_z = lax.ppermute(cotangent, "mp", mp_perm(2))
    f_c = lax.ppermute(frames, "mp", mp_perm(1))
    c_c = lax.ppermute(cotangent, "mp", mp_perm(1))
    w_z = lax.all_gather(piece, "dp", axis_index_groups=XY_GROUPS, axis=0, tiled=True)
    f_d = lax.ppermute(f_z, "mp", mp_perm(1))
    c_d = lax.ppermute(c_z, "mp", mp_perm(1))

    prod = pltpu.VMEM((FR, 3, 9 * OWN, PIX), F32)
    maps = pltpu.VMEM((FR, CH, PIX), BF16)
    big = 2 * TAPS * OWN * CH * FR * PIX
    pre, hidden, ordered = call(
        first_conv,
        (shape((FR, OWN, PIX), F32), shape((FR, OWN, PIX), BF16), shape((FR, CH, PIX), BF16)),
        [maps, prod], (meta, frames, f_c, f_z, f_d, first_weight), big,
    )
    h_z = lax.ppermute(hidden, "mp", mp_perm(2))
    h_c = lax.ppermute(hidden, "mp", mp_perm(1))
    h_d = lax.ppermute(h_z, "mp", mp_perm(1))

    sent = shape((TAPS, 16, CH), BF16)
    *sends, own = call(
        second_grad_part,
        (sent, sent, sent, shape((TAPS, 16, CH), F32)),
        [maps, pltpu.VMEM((FR, 9 * OWN, PIX), BF16), pltpu.VMEM((TAPS, OWN, CH), F32)],
        (meta, cotangent, c_c, c_z, c_d, hidden), big,
    )
    got = [
        lax.ppermute(s, "dp", dp_perm(lambda z, y, x, r=r: (z, (y + r) % 4, x)))
        for r, s in zip((1, 2, 3), sends)
    ]

    g_keep, g_send = call(
        hidden_grad_part,
        (shape((FR, OWN, PIX), F32),) * 2,
        [
            pltpu.VMEM((2, 9 * OWN, PIX), BF16),
            pltpu.VMEM((2, 3, 128, 9 * OWN), BF16),
            pltpu.VMEM((FR, 128, PIX), F32),
        ],
        (meta, cotangent, c_z, second_weight, w_z), big,
    )
    g_got = lax.ppermute(g_send, "mp", mp_perm(1))

    sent = shape((64, LANES), BF16)
    *sends1, own1 = call(
        first_grad_part,
        (sent, sent, sent, shape((64, LANES), F32)),
        [pltpu.VMEM((9 * OWN, FR * PIX), BF16), pltpu.VMEM((CH, LANES), F32)],
        (meta, pre, g_keep, g_got, ordered), big,
    )
    got1 = [
        lax.ppermute(s, "dp", dp_perm(lambda z, y, x, r=r: (z, y, (x + r) % 4)))
        for r, s in zip((1, 2, 3), sends1)
    ]

    sent = shape((4, 32, CH), BF16)
    *sends, own = call(
        second_grad_x,
        (sent, sent, sent, shape((4, 32, CH), F32)),
        [pltpu.VMEM((2, 512, 128), F32)],
        (meta, own, *got),
    )
    got = [
        lax.ppermute(s, "dp", dp_perm(lambda z, y, x, r=r: (z, y, (x + r) % 4)))
        for r, s in zip((1, 2, 3), sends)
    ]
    sent = shape((16, LANES), BF16)
    *sends1, own1 = call(
        first_grad_y,
        (sent, sent, sent, shape((16, LANES), F32)),
        [pltpu.VMEM((64, LANES), F32)],
        (meta, own1, *got1),
    )
    got1 = [
        lax.ppermute(s, "dp", dp_perm(lambda z, y, x, r=r: (z, (y + r) % 4, x)))
        for r, s in zip((1, 2, 3), sends1)
    ]

    parts = call(
        second_grad_z,
        (shape((2, 32, 128), F32),) * 4,
        [pltpu.VMEM((2, 4, 32, 128), F32)],
        (meta, own, *got),
    )
    parts = [
        lax.ppermute(p, ("dp", "mp"), all_perm(lambda z, y, x, m, r=r: (m, y, x, z ^ r)))
        for r, p in enumerate(parts)
    ]
    own1, *sends1 = call(first_grad_z, (shape((4, LANES), F32),) * 4, [], (meta, own1, *got1))
    got1 = [
        lax.ppermute(s, "dp", dp_perm(lambda z, y, x, r=r: ((z + r) % 4, y, x)))
        for r, s in zip((1, 2, 3), sends1)
    ]

    output = call(
        second_conv,
        shape((FR, OWN, PIX), BF16),
        [maps, prod], (meta, hidden, h_c, h_z, h_d, second_weight, frames), big,
    )

    second = parts[0] + parts[1] + parts[2] + parts[3]
    second = second[:, :TAPS].reshape(2, TAPS, 2, OWN).transpose(1, 3, 2, 0).reshape(TAPS, OWN, 4)
    first = own1 + got1[0] + got1[1] + got1[2]
    first = first[:, :TAPS * OWN].reshape(4, TAPS, OWN).transpose(1, 2, 0)
    return output, first, second


def solution(mesh):
    in_specs = (
        P("dp", "mp", None),
        P("dp"),
        P(None, "mp", None),
        P(None, "mp", None),
        P("dp", "mp", None),
    )
    out_specs = (P("dp", "mp", None), P(None, "mp", "dp"), P(None, "mp", "dp"))
    return jax.shard_map(local, mesh=mesh, in_specs=in_specs, out_specs=out_specs, check_vma=False)
```

```python
import functools

import jax
import jax.numpy as jnp
from jax import lax
from jax.experimental import pallas as pl
from jax.experimental.pallas import tpu as pltpu
from jax.sharding import PartitionSpec as P

F32, BF16 = jnp.float32, jnp.bfloat16
SIDE, PIX, FR, CH, OWN, TAPS = 16, 256, 4, 256, 64, 27
STEPS = tuple((u, v) for u in (-1, 0, 1) for v in (-1, 0, 1))
LANES = 1792


def place(zl, y, x):
    return (zl * 4 + y) * 4 + x


def dp_perm(move):
    return [
        (place(z, y, x), place(*move(z, y, x)))
        for z in range(4) for y in range(4) for x in range(4)
    ]


def all_perm(move):
    pairs = []
    for z in range(4):
        for y in range(4):
            for x in range(4):
                for m in range(4):
                    z2, y2, x2, m2 = move(z, y, x, m)
                    pairs.append((place(z, y, x) * 4 + m, place(z2, y2, x2) * 4 + m2))
    return pairs


def mp_perm(flip):
    return [(m, m ^ flip) for m in range(4)]


def call(kernel, outs, scratch, args, flops=0, after=()):
    specs = [pl.BlockSpec(memory_space=pltpu.SMEM)]
    specs += [pl.BlockSpec(memory_space=pltpu.VMEM)] * (len(args) - 1)
    specs += [pl.BlockSpec(memory_space=pl.ANY)] * len(after)
    size = sum(a.size * a.dtype.itemsize for a in args)
    n = len(args)

    def body(*refs):
        kernel(*refs[:n], *refs[n + len(after):])

    return pl.pallas_call(
        body,
        out_shape=outs,
        in_specs=specs,
        out_specs=jax.tree.map(lambda _: pl.BlockSpec(memory_space=pltpu.VMEM), outs),
        scratch_shapes=scratch,
        cost_estimate=pl.CostEstimate(flops=flops, bytes_accessed=size, transcendentals=0),
        compiler_params=pltpu.CompilerParams(vmem_limit_bytes=48 * 2**20),
    )(*args, *after)


def shape(dims, kind):
    return jax.ShapeDtypeStruct(dims, kind)


def inside(u, v):
    pos = lax.broadcasted_iota(jnp.int32, (1, PIX), 1)
    row, col = pos >> 4, pos & 15
    ok = (row + u >= 0) & (row + u < SIDE) & (col + v >= 0) & (col + v < SIDE)
    return jnp.where(ok, 1.0, 0.0).astype(F32)


def turn(value, step):
    return value if step % PIX == 0 else pltpu.roll(value, step % PIX, 1)


def source(meta, f, lag):
    return f - jnp.minimum(jnp.maximum(meta[f], 0), lag)


def nt(a, b):
    return lax.dot_general(a, b, (((1,), (1,)), ((), ())), preferred_element_type=F32)


def nn(a, b):
    return lax.dot_general(a, b, (((1,), (0,)), ((), ())), preferred_element_type=F32)


def rows(start, size):
    return pl.ds(pl.multiple_of(start, size), size)


def gather_rows(meta, pieces, out, live=False):
    m = meta[7]
    for f in range(FR):
        for flip, piece in enumerate(pieces):
            value = piece[f]
            if live:
                value = (value.astype(F32) * jnp.where(meta[f] >= 0, 1.0, 0.0)).astype(BF16)
            out[f, rows((m ^ flip) * OWN, OWN), :] = value


def conv_into(meta, weight, maps, wide, prod, finish):
    for lag in range(3):
        wide[:, lag * CH:(lag + 1) * CH] = weight[9 * lag:9 * lag + 9].reshape(9 * OWN, CH)
    for f in range(FR):
        seen = jnp.concatenate([maps[source(meta, f, lag)] for lag in range(3)], axis=0)
        prod[f] = nn(wide[...], seen)
        total = jnp.zeros((OWN, PIX), F32)
        for i, (u, v) in enumerate(STEPS):
            total = total + turn(prod[f, i * OWN:(i + 1) * OWN, :], -(SIDE * u + v)) * inside(u, v)
        finish(f, total)


def first_conv(meta, f0, f1, f2, f3, weight, pre, hidden, ordered, maps, wide, prod):
    gather_rows(meta, (f0, f1, f2, f3), maps)

    def finish(f, total):
        pre[f] = total
        hidden[f] = (total / (1.0 + jnp.exp(-total))).astype(BF16)
    conv_into(meta, weight, maps, wide, prod, finish)
    r = lax.broadcasted_iota(jnp.int32, (CH, CH), 0)
    c = lax.broadcasted_iota(jnp.int32, (CH, CH), 1)
    want = ((r >> 2) & 3) * 64 + ((r >> 4) & 3) * 16 + (r >> 6) * 4 + (r & 3)
    pick = jnp.where(c == want, 1.0, 0.0).astype(BF16)
    for f in range(FR):
        ordered[f] = nn(pick, maps[f]).astype(BF16)


def second_conv(meta, h0, h1, h2, h3, weight, frames, out, maps, wide, prod):
    gather_rows(meta, (h0, h1, h2, h3), maps)

    def finish(f, total):
        out[f] = (frames[f].astype(F32) + total).astype(BF16)
    conv_into(meta, weight, maps, wide, prod, finish)


def second_grad_part(meta, c0, c1, c2, c3, hidden, s1, s2, s3, own, maps, taps, total):
    gather_rows(meta, (c0, c1, c2, c3), maps, live=True)
    for f in range(FR):
        h = hidden[f].astype(F32)
        for i, (u, v) in enumerate(STEPS):
            taps[f, i * OWN:(i + 1) * OWN, :] = (turn(h, -(SIDE * u + v)) * inside(u, v)).astype(BF16)
    cot = jnp.concatenate([maps[f] for f in range(FR)], axis=1)
    lhs = jnp.concatenate([
        jnp.concatenate([taps[source(meta, f, lag)] for f in range(FR)], axis=1) for lag in range(3)
    ], axis=0)
    total[...] = nt(lhs, cot).reshape(TAPS, OWN, CH)
    y = meta[5]
    own[...] = total[:, rows(y * 16, 16), :]
    for r, out in ((1, s1), (2, s2), (3, s3)):
        out[...] = total[:, rows(((y + r) & 3) * 16, 16), :].astype(BF16)


def hidden_grad_part(meta, cot, weight, keep, send, taps, flipped, total):
    core = meta[7] & 1
    eye = jnp.where(
        lax.broadcasted_iota(jnp.int32, (CH, CH), 0) == lax.broadcasted_iota(jnp.int32, (CH, CH), 1),
        1.0, 0.0,
    ).astype(BF16)
    for lag in range(3):
        flipped[lag * CH:(lag + 1) * CH, :] = nt(eye, weight[9 * lag:9 * lag + 9].reshape(9 * OWN, CH)).astype(BF16)
    total[...] = jnp.zeros(total.shape, F32)

    def slot(f, _):
        g = cot[f].astype(F32) * jnp.where(meta[f] >= 0, 1.0, 0.0)
        for i, (u, v) in enumerate(STEPS):
            taps[i * OWN:(i + 1) * OWN, :] = turn(g * inside(u, v), SIDE * u + v).astype(BF16)
        terms = nn(flipped[...], taps[...])
        for lag in range(3):
            at = source(meta, f, lag)
            total[at] = total[at] + terms[lag * CH:(lag + 1) * CH]
        return 0
    lax.fori_loop(0, FR, slot, 0)
    for half in range(2):
        keep[half] = total[:, rows(half * 128 + core * OWN, OWN), :]
        send[half] = total[:, rows(half * 128 + (1 - core) * OWN, OWN), :]


def hidden_grad_add(meta, keep, got, mine, send):
    half = meta[7] >> 1
    mine[...] = keep[half] + got[half]
    send[...] = keep[1 - half] + got[1 - half]


def first_grad_part(meta, pre, ha, hb, ordered, s1, s2, s3, own, taps, total):
    for f in range(FR):
        p = pre[f]
        sigma = 1.0 / (1.0 + jnp.exp(-p))
        g = ((ha[f] + hb[f]) * sigma * (1.0 + p * (1.0 - sigma))).astype(BF16).astype(F32)
        for i, (u, v) in enumerate(STEPS):
            taps[i * OWN:(i + 1) * OWN, f * PIX:(f + 1) * PIX] = turn(g * inside(u, v), SIDE * u + v).astype(BF16)
    lhs = jnp.concatenate([
        jnp.concatenate([ordered[source(meta, f, lag)] for f in range(FR)], axis=1) for lag in range(3)
    ], axis=0)
    both = nt(lhs, taps[...])
    for lag in range(3):
        total[:, 576 * lag:576 * lag + 576] = both[lag * CH:(lag + 1) * CH]
    total[:, 1728:LANES] = jnp.zeros((CH, LANES - 1728), F32)
    x = meta[6]
    own[...] = total[rows(x * 64, 64), :]
    for r, out in ((1, s1), (2, s2), (3, s3)):
        out[...] = total[rows(((x + r) & 3) * 64, 64), :].astype(BF16)


def first_grad_y(meta, own, r1, r2, r3, s1, s2, s3, keep, total):
    total[...] = own[...] + r1[...].astype(F32) + r2[...].astype(F32) + r3[...].astype(F32)
    y = meta[5]
    keep[...] = total[rows(y * 16, 16), :]
    for r, out in ((1, s1), (2, s2), (3, s3)):
        out[...] = total[rows(((y + r) & 3) * 16, 16), :].astype(BF16)


def second_grad_x(meta, own, r1, r2, r3, s1, s2, s3, keep, total):
    for h in range(2):
        lane = slice(128 * h, 128 * h + 128)
        value = own[:, :, lane] + r1[:, :, lane].astype(F32) + r2[:, :, lane].astype(F32) + r3[:, :, lane].astype(F32)
        total[h, 0:432, :] = value.reshape(432, 128)
        total[h, 432:512, :] = jnp.zeros((80, 128), F32)
    for r, out in ((0, keep), (1, s1), (2, s2), (3, s3)):
        x = (meta[6] + r) & 3
        for i in range(4):
            for h in range(2):
                value = total[h, pl.ds(x * 4 + i, 32, stride=16), :]
                out[i, :, 128 * h:128 * h + 128] = value.astype(out.dtype)


def pack_z(meta, own1, a1, a2, a3, own2, b1, b2, b3, keep, s1, s2, s3, out):
    total = own1[...] + a1[...].astype(F32) + a2[...].astype(F32) + a3[...].astype(F32)
    for z in range(4):
        for j in range(14):
            out[z, 4 * j:4 * j + 4, :] = total[4 * z:4 * z + 4, 128 * j:128 * j + 128]
    low = lax.broadcasted_iota(jnp.int32, (32, 128), 1) < 64
    for h in range(2):
        lane = slice(128 * h, 128 * h + 128)
        total = own2[:, :, lane] + b1[:, :, lane].astype(F32) + b2[:, :, lane].astype(F32) + b3[:, :, lane].astype(F32)
        for j in range(2):
            a, b = total[j], total[j + 2]
            part = slice(56 + 32 * j, 88 + 32 * j)
            out[2 * h, part, :] = jnp.where(low, a, pltpu.roll(b, 64, 1))
            out[2 * h + 1, part, :] = jnp.where(low, pltpu.roll(a, 64, 1), b)
    for r, ref in enumerate((keep, s1, s2, s3)):
        ref[...] = out[(meta[4] + r) & 3]


def add_z(meta, own, a1, a2, a3, first, second):
    for t in range(TAPS):
        part = slice(4 * (t // 2), 4 * (t // 2) + 4)
        value = own[part, :] + a1[part, :] + a2[part, :] + a3[part, :]
        first[t] = value[:, 64 * (t % 2):64 * (t % 2) + 64]
    second[...] = own[56:120, :] + a1[56:120, :] + a2[56:120, :] + a3[56:120, :]


def ring(value, axis):
    moves = {
        "x": lambda k: lambda z, y, x: (z, y, (x + k) % 4),
        "y": lambda k: lambda z, y, x: (z, (y + k) % 4, x),
        "z": lambda k: lambda z, y, x: ((z + k) % 4, y, x),
    }
    values = value if isinstance(value, (list, tuple)) else [value] * 3
    return [lax.ppermute(v, "dp", dp_perm(moves[axis](k))) for k, v in zip((1, 2, 3), values)]


def behind(value, other):
    return lax.optimization_barrier((value, other))[0]


def local(frames, frame_offsets, first_weight, second_weight, cotangent):
    d, m = lax.axis_index("dp"), lax.axis_index("mp")
    zl, y, x = d // 16, (d // 4) % 4, d % 4
    meta = jnp.concatenate([frame_offsets, jnp.stack([zl, y, x, m]).astype(jnp.int32)])

    big = 2 * TAPS * OWN * CH * FR * PIX
    f_z = lax.ppermute(frames, "mp", mp_perm(2))
    f_c = lax.ppermute(frames, "mp", mp_perm(1))
    c_c = lax.ppermute(cotangent, "mp", mp_perm(1))
    halves = shape((2, FR, OWN, PIX), F32)
    g_keep, g_send = call(
        hidden_grad_part,
        (halves, halves),
        [pltpu.VMEM((9 * OWN, PIX), BF16), pltpu.VMEM((3 * CH, 9 * OWN), BF16), pltpu.VMEM((FR, CH, PIX), F32)],
        (meta, cotangent, second_weight), big,
    )
    g_got = lax.ppermute(behind(g_send, f_z), "mp", mp_perm(1))
    g_keep, g_send = call(hidden_grad_add, (shape((FR, OWN, PIX), F32),) * 2, [], (meta, g_keep, g_got))
    f_d = lax.ppermute(f_z, "mp", mp_perm(1))
    c_z = lax.ppermute(behind(cotangent, f_z), "mp", mp_perm(2))
    c_d = lax.ppermute(c_z, "mp", mp_perm(1))
    g_got = lax.ppermute(behind(g_send, c_z), "mp", mp_perm(2))

    prod = pltpu.VMEM((FR, 9 * OWN, PIX), F32)
    wide = pltpu.VMEM((9 * OWN, 3 * CH), BF16)
    maps = pltpu.VMEM((FR, CH, PIX), BF16)
    pre, hidden, ordered = call(
        first_conv,
        (shape((FR, OWN, PIX), F32), shape((FR, OWN, PIX), BF16), shape((FR, CH, PIX), BF16)),
        [maps, wide, prod], (meta, frames, f_c, f_z, f_d, first_weight), big,
    )
    h_z = lax.ppermute(behind(hidden, g_got), "mp", mp_perm(2))
    h_c = lax.ppermute(hidden, "mp", mp_perm(1))
    h_d = lax.ppermute(h_z, "mp", mp_perm(1))

    sent = shape((TAPS, 16, CH), BF16)
    *sends, own = call(
        second_grad_part,
        (sent, sent, sent, shape((TAPS, 16, CH), F32)),
        [maps, pltpu.VMEM((FR, 9 * OWN, PIX), BF16), pltpu.VMEM((TAPS, OWN, CH), F32)],
        (meta, cotangent, c_c, c_z, c_d, hidden), big,
    )
    got = ring(sends, "y")

    sent = shape((64, LANES), BF16)
    *sends1, own1 = call(
        first_grad_part,
        (sent, sent, sent, shape((64, LANES), F32)),
        [pltpu.VMEM((9 * OWN, FR * PIX), BF16), pltpu.VMEM((CH, LANES), F32)],
        (meta, pre, g_keep, g_got, ordered), big,
    )
    got1 = ring(sends1, "x")

    output = call(
        second_conv,
        shape((FR, OWN, PIX), BF16),
        [maps, wide, prod], (meta, hidden, h_c, h_z, h_d, second_weight, frames), big, after=(own1,),
    )

    sent = shape((4, 32, CH), BF16)
    *sends, own = call(
        second_grad_x,
        (sent, sent, sent, shape((4, 32, CH), F32)),
        [pltpu.VMEM((2, 512, 128), F32)],
        (meta, own, *got),
    )
    got = ring(sends, "x")
    sent = shape((16, LANES), BF16)
    *sends1, own1 = call(
        first_grad_y,
        (sent, sent, sent, shape((16, LANES), F32)),
        [pltpu.VMEM((64, LANES), F32)],
        (meta, own1, *got1), after=(output,),
    )
    got1 = ring(sends1, "y")

    sum_z = shape((120, 128), F32)
    own, *sends = call(pack_z, (sum_z,) * 4, [pltpu.VMEM((4, 120, 128), F32)], (meta, own1, *got1, own, *got))
    got = ring(sends, "z")
    first, second = call(add_z, (shape((TAPS, 4, OWN), F32), shape((64, 128), F32)), [], (meta, own, *got))
    second = lax.ppermute(second, ("dp", "mp"), all_perm(lambda z, y, x, m: (m, y, x, z)))

    second = second.reshape(2, 32, 2, OWN)[:, :TAPS].transpose(1, 3, 2, 0).reshape(TAPS, OWN, 4)
    first = first.transpose(0, 2, 1)
    return output, first, second


def solution(mesh):
    in_specs = (
        P("dp", "mp", None),
        P("dp"),
        P(None, "mp", None),
        P(None, "mp", None),
        P("dp", "mp", None),
    )
    out_specs = (P("dp", "mp", None), P(None, "mp", "dp"), P(None, "mp", "dp"))
    return jax.shard_map(local, mesh=mesh, in_specs=in_specs, out_specs=out_specs, check_vma=False)
```

```python
import functools

import jax
import jax.numpy as jnp
from jax import lax
from jax.experimental import pallas as pl
from jax.experimental.pallas import tpu as pltpu
from jax.sharding import PartitionSpec as P

F32, BF16 = jnp.float32, jnp.bfloat16
SIDE, PIX, FR, CH, OWN, TAPS = 16, 256, 4, 256, 64, 27
STEPS = tuple((u, v) for u in (-1, 0, 1) for v in (-1, 0, 1))
LANES = 1792


def place(zl, y, x):
    return (zl * 4 + y) * 4 + x


def dp_perm(move):
    return [
        (place(z, y, x), place(*move(z, y, x)))
        for z in range(4) for y in range(4) for x in range(4)
    ]


def mp_perm(flip):
    return [(m, m ^ flip) for m in range(4)]


def call(kernel, outs, scratch, args, flops=0, after=()):
    specs = [pl.BlockSpec(memory_space=pltpu.SMEM)]
    specs += [pl.BlockSpec(memory_space=pltpu.VMEM)] * (len(args) - 1)
    specs += [pl.BlockSpec(memory_space=pl.ANY)] * len(after)
    size = sum(a.size * a.dtype.itemsize for a in args)
    n = len(args)

    def body(*refs):
        kernel(*refs[:n], *refs[n + len(after):])

    return pl.pallas_call(
        body,
        out_shape=outs,
        in_specs=specs,
        out_specs=jax.tree.map(lambda _: pl.BlockSpec(memory_space=pltpu.VMEM), outs),
        scratch_shapes=scratch,
        cost_estimate=pl.CostEstimate(flops=flops, bytes_accessed=size, transcendentals=0),
        compiler_params=pltpu.CompilerParams(vmem_limit_bytes=48 * 2**20),
    )(*args, *after)


def shape(dims, kind):
    return jax.ShapeDtypeStruct(dims, kind)


def inside(u, v):
    pos = lax.broadcasted_iota(jnp.int32, (1, PIX), 1)
    row, col = pos >> 4, pos & 15
    ok = (row + u >= 0) & (row + u < SIDE) & (col + v >= 0) & (col + v < SIDE)
    return jnp.where(ok, 1.0, 0.0).astype(F32)


def turn(value, step):
    return value if step % PIX == 0 else pltpu.roll(value, step % PIX, 1)


def source(meta, f, lag):
    return f - jnp.minimum(jnp.maximum(meta[f], 0), lag)


def nt(a, b):
    return lax.dot_general(a, b, (((1,), (1,)), ((), ())), preferred_element_type=F32)


def nn(a, b):
    return lax.dot_general(a, b, (((1,), (0,)), ((), ())), preferred_element_type=F32)


def rows(start, size):
    return pl.ds(pl.multiple_of(start, size), size)


def gather_rows(meta, pieces, out, live=False):
    m = meta[7]
    for f in range(FR):
        for flip, piece in enumerate(pieces):
            value = piece[f]
            if live:
                value = (value.astype(F32) * jnp.where(meta[f] >= 0, 1.0, 0.0)).astype(BF16)
            out[f, rows((m ^ flip) * OWN, OWN), :] = value


def conv_into(meta, weight, maps, wide, prod, finish):
    for lag in range(3):
        wide[:, lag * CH:(lag + 1) * CH] = weight[9 * lag:9 * lag + 9].reshape(9 * OWN, CH)
    for f in range(FR):
        seen = jnp.concatenate([maps[source(meta, f, lag)] for lag in range(3)], axis=0)
        prod[f] = nn(wide[...], seen)
        total = jnp.zeros((OWN, PIX), F32)
        for i, (u, v) in enumerate(STEPS):
            total = total + turn(prod[f, i * OWN:(i + 1) * OWN, :], -(SIDE * u + v)) * inside(u, v)
        finish(f, total)


def first_conv(meta, f0, f1, f2, f3, weight, pre, hidden, ordered, maps, wide, prod):
    gather_rows(meta, (f0, f1, f2, f3), maps)

    def finish(f, total):
        pre[f] = total
        hidden[f] = (total / (1.0 + jnp.exp(-total))).astype(BF16)
    conv_into(meta, weight, maps, wide, prod, finish)
    for f in range(FR):
        ordered[f] = arrange(maps[f], "x")


def arrange(value, axis):
    r = lax.broadcasted_iota(jnp.int32, (CH, CH), 0)
    c = lax.broadcasted_iota(jnp.int32, (CH, CH), 1)
    high, low = (4, 16) if axis == "x" else (16, 4)
    want = ((r >> 2) & 3) * 64 + (r >> 6) * high + ((r >> 4) & 3) * low + (r & 3)
    return nn(jnp.where(c == want, 1.0, 0.0).astype(BF16), value).astype(BF16)


def second_conv(meta, h0, h1, h2, h3, weight, frames, out, maps, wide, prod):
    gather_rows(meta, (h0, h1, h2, h3), maps)

    def finish(f, total):
        out[f] = (frames[f].astype(F32) + total).astype(BF16)
    conv_into(meta, weight, maps, wide, prod, finish)


def cut_grad(meta, ordered, taps, at, sends, own, total):
    lhs = jnp.concatenate([
        jnp.concatenate([ordered[source(meta, f, lag)] for f in range(FR)], axis=1) for lag in range(3)
    ], axis=0)
    both = nt(lhs, taps[...])
    for lag in range(3):
        total[:, 576 * lag:576 * lag + 576] = both[lag * CH:(lag + 1) * CH]
    total[:, 1728:LANES] = jnp.zeros((CH, LANES - 1728), F32)
    own[...] = total[rows(at * 64, 64), :]
    for r, out in zip((1, 2, 3), sends):
        out[...] = total[rows(((at + r) & 3) * 64, 64), :].astype(BF16)


def second_grad_part(meta, h0, h1, h2, h3, taps, s1, s2, s3, own, maps, ordered, total):
    gather_rows(meta, (h0, h1, h2, h3), maps)
    for f in range(FR):
        ordered[f] = arrange(maps[f], "y")
    cut_grad(meta, ordered, taps, meta[5], (s1, s2, s3), own, total)


def hidden_grad_part(meta, cot, c_core, weight, w_core, keep, send, taps, both, flipped, total):
    core, half = meta[7] & 1, meta[7] >> 1
    r = lax.broadcasted_iota(jnp.int32, (128, CH), 0)
    c = lax.broadcasted_iota(jnp.int32, (128, CH), 1)
    want = jnp.where(r < OWN, half, 1 - half) * 128 + core * OWN + (r & 63)
    pick = jnp.where(c == want, 1.0, 0.0).astype(BF16)
    for who, ref in enumerate((weight, w_core)):
        for lag in range(3):
            w = ref[9 * lag:9 * lag + 9].reshape(9 * OWN, CH)
            flipped[lag * 128:(lag + 1) * 128, who * 576:(who + 1) * 576] = nt(pick, w).astype(BF16)
    total[...] = jnp.zeros(total.shape, F32)
    for f in range(FR):
        live = jnp.where(meta[f] >= 0, 1.0, 0.0)
        for who, ref in enumerate((cot, c_core)):
            g = ref[f].astype(F32) * live
            for i, (u, v) in enumerate(STEPS):
                at = (who * 9 + i) * OWN
                both[at:at + OWN, :] = turn(g * inside(u, v), SIDE * u + v).astype(BF16)
        taps[:, f * PIX:(f + 1) * PIX] = both[0:9 * OWN, :]
        terms = nn(flipped[...], both[...])
        for lag in range(3):
            at = source(meta, f, lag)
            total[at] = total[at] + terms[lag * 128:(lag + 1) * 128]
    keep[...] = total[:, 0:OWN, :]
    send[...] = total[:, OWN:128, :]


def first_grad_part(meta, pre, ha, hb, ordered, s1, s2, s3, own, taps, total):
    for f in range(FR):
        p = pre[f]
        sigma = 1.0 / (1.0 + jnp.exp(-p))
        g = ((ha[f] + hb[f]) * sigma * (1.0 + p * (1.0 - sigma))).astype(BF16).astype(F32)
        for i, (u, v) in enumerate(STEPS):
            taps[i * OWN:(i + 1) * OWN, f * PIX:(f + 1) * PIX] = turn(g * inside(u, v), SIDE * u + v).astype(BF16)
    cut_grad(meta, ordered, taps, meta[6], (s1, s2, s3), own, total)


def cut_again(which, meta, own, r1, r2, r3, s1, s2, s3, keep, total):
    total[...] = own[...] + r1[...].astype(F32) + r2[...].astype(F32) + r3[...].astype(F32)
    at = meta[which]
    keep[...] = total[rows(at * 16, 16), :]
    for r, out in ((1, s1), (2, s2), (3, s3)):
        out[...] = total[rows(((at + r) & 3) * 16, 16), :].astype(BF16)


def pack_z(meta, own1, a1, a2, a3, own2, b1, b2, b3, keep, s1, s2, s3, out):
    for g, (own, r1, r2, r3) in enumerate(((own1, a1, a2, a3), (own2, b1, b2, b3))):
        total = own[...] + r1[...].astype(F32) + r2[...].astype(F32) + r3[...].astype(F32)
        for z in range(4):
            for j in range(14):
                out[z, 56 * g + 4 * j:56 * g + 4 * j + 4, :] = total[4 * z:4 * z + 4, 128 * j:128 * j + 128]
    for r, ref in enumerate((keep, s1, s2, s3)):
        ref[...] = out[(meta[4] + r) & 3]


def add_z(meta, own, a1, a2, a3, first, second):
    for g, out in enumerate((first, second)):
        for t in range(TAPS):
            part = slice(56 * g + 4 * (t // 2), 56 * g + 4 * (t // 2) + 4)
            value = own[part, :] + a1[part, :] + a2[part, :] + a3[part, :]
            out[t] = value[:, 64 * (t % 2):64 * (t % 2) + 64]


def ring(value, axis):
    moves = {
        "x": lambda k: lambda z, y, x: (z, y, (x + k) % 4),
        "y": lambda k: lambda z, y, x: (z, (y + k) % 4, x),
        "z": lambda k: lambda z, y, x: ((z + k) % 4, y, x),
    }
    values = value if isinstance(value, (list, tuple)) else [value] * 3
    return [lax.ppermute(v, "dp", dp_perm(moves[axis](k))) for k, v in zip((1, 2, 3), values)]


def behind(value, other):
    return lax.optimization_barrier((value, other))[0]


def local(frames, frame_offsets, first_weight, second_weight, cotangent):
    d, m = lax.axis_index("dp"), lax.axis_index("mp")
    zl, y, x = d // 16, (d // 4) % 4, d % 4
    meta = jnp.concatenate([frame_offsets, jnp.stack([zl, y, x, m]).astype(jnp.int32)])

    big = 2 * TAPS * OWN * CH * FR * PIX
    one = shape((FR, OWN, PIX), F32)
    f_z = lax.ppermute(frames, "mp", mp_perm(2))
    f_c = lax.ppermute(frames, "mp", mp_perm(1))
    c_c = lax.ppermute(cotangent, "mp", mp_perm(1))
    w_c = lax.ppermute(second_weight, "mp", mp_perm(1))
    g_keep, g_send, taps = call(
        hidden_grad_part,
        (one, one, shape((9 * OWN, FR * PIX), BF16)),
        [pltpu.VMEM((18 * OWN, PIX), BF16), pltpu.VMEM((3 * 128, 18 * OWN), BF16), pltpu.VMEM((FR, 128, PIX), F32)],
        (meta, cotangent, c_c, second_weight, w_c), big,
    )
    g_got = lax.ppermute(behind(g_send, f_z), "mp", mp_perm(2))
    f_d = lax.ppermute(f_z, "mp", mp_perm(1))

    prod = pltpu.VMEM((FR, 9 * OWN, PIX), F32)
    wide = pltpu.VMEM((9 * OWN, 3 * CH), BF16)
    maps = pltpu.VMEM((FR, CH, PIX), BF16)
    pre, hidden, ordered = call(
        first_conv,
        (one, shape((FR, OWN, PIX), BF16), shape((FR, CH, PIX), BF16)),
        [maps, wide, prod], (meta, frames, f_c, f_z, f_d, first_weight), big, after=(g_send,),
    )
    h_z = lax.ppermute(hidden, "mp", mp_perm(2))
    h_c = lax.ppermute(hidden, "mp", mp_perm(1))

    sent, held = (shape((64, LANES), BF16),) * 3, shape((64, LANES), F32)
    total = pltpu.VMEM((CH, LANES), F32)
    *sends1, own1 = call(
        first_grad_part, (*sent, held), [pltpu.VMEM((9 * OWN, FR * PIX), BF16), total],
        (meta, pre, g_keep, g_got, ordered), big,
    )
    got1 = ring(sends1, "x")

    h_d = lax.ppermute(h_z, "mp", mp_perm(1))
    *sends2, own2 = call(
        second_grad_part, (*sent, held), [maps, maps, total], (meta, hidden, h_c, h_z, h_d, taps), big, after=(own1,),
    )
    got2 = ring(sends2, "y")

    sent, held = (shape((16, LANES), BF16),) * 3, shape((16, LANES), F32)
    total = pltpu.VMEM((64, LANES), F32)
    output = call(
        second_conv,
        shape((FR, OWN, PIX), BF16),
        [maps, wide, prod], (meta, hidden, h_c, h_z, h_d, second_weight, frames), big, after=(own2,),
    )
    *sends1, own1 = call(functools.partial(cut_again, 5), (*sent, held), [total], (meta, own1, *got1), after=(output,))
    got1 = ring(sends1, "y")
    *sends2, own2 = call(functools.partial(cut_again, 6), (*sent, held), [total], (meta, own2, *got2), after=(own1,))
    got2 = ring(sends2, "x")

    sum_z = shape((112, 128), F32)
    own, *sends = call(pack_z, (sum_z,) * 4, [pltpu.VMEM((4, 112, 128), F32)], (meta, own1, *got1, own2, *got2))
    got = ring(sends, "z")
    first, second = call(add_z, (shape((TAPS, 4, OWN), F32),) * 2, [], (meta, own, *got))
    first, second = first.transpose(0, 2, 1), second.transpose(0, 2, 1)
    return output, first, second


def solution(mesh):
    in_specs = (
        P("dp", "mp", None),
        P("dp"),
        P(None, "mp", None),
        P(None, "mp", None),
        P("dp", "mp", None),
    )
    out_specs = (P("dp", "mp", None), P(None, "mp", "dp"), P(None, "mp", "dp"))
    return jax.shard_map(local, mesh=mesh, in_specs=in_specs, out_specs=out_specs, check_vma=False)
```

```python
import jax
import jax.numpy as jnp
from jax import lax
from jax.experimental import pallas as pl
from jax.experimental.pallas import tpu as pltpu
from jax.sharding import PartitionSpec as P

F32, BF16 = jnp.float32, jnp.bfloat16
SIDE, PIX, FR, CH, OWN, TAPS = 16, 256, 4, 256, 64, 27
STEPS = tuple((u, v) for u in (-1, 0, 1) for v in (-1, 0, 1))
LANES = 1792


def place(zl, y, x):
    return (zl * 4 + y) * 4 + x


def dp_perm(move):
    return [
        (place(z, y, x), place(*move(z, y, x)))
        for z in range(4) for y in range(4) for x in range(4)
    ]


def mp_perm(flip):
    return [(m, m ^ flip) for m in range(4)]


def call(kernel, outs, scratch, args, flops=0, after=()):
    specs = [pl.BlockSpec(memory_space=pltpu.SMEM)]
    specs += [pl.BlockSpec(memory_space=pltpu.VMEM)] * (len(args) - 1)
    specs += [pl.BlockSpec(memory_space=pl.ANY)] * len(after)
    size = sum(a.size * a.dtype.itemsize for a in args)
    n = len(args)

    def body(*refs):
        kernel(*refs[:n], *refs[n + len(after):])

    return pl.pallas_call(
        body,
        out_shape=outs,
        in_specs=specs,
        out_specs=jax.tree.map(lambda _: pl.BlockSpec(memory_space=pltpu.VMEM), outs),
        scratch_shapes=scratch,
        cost_estimate=pl.CostEstimate(flops=flops, bytes_accessed=size, transcendentals=0),
        compiler_params=pltpu.CompilerParams(vmem_limit_bytes=48 * 2**20),
    )(*args, *after)


def shape(dims, kind):
    return jax.ShapeDtypeStruct(dims, kind)


def inside(u, v):
    pos = lax.broadcasted_iota(jnp.int32, (1, PIX), 1)
    row, col = pos >> 4, pos & 15
    ok = (row + u >= 0) & (row + u < SIDE) & (col + v >= 0) & (col + v < SIDE)
    return jnp.where(ok, 1.0, 0.0).astype(F32)


def turn(value, step):
    return value if step % PIX == 0 else pltpu.roll(value, step % PIX, 1)


def source(meta, f, lag):
    return f - jnp.minimum(jnp.maximum(meta[f], 0), lag)


def nt(a, b):
    return lax.dot_general(a, b, (((1,), (1,)), ((), ())), preferred_element_type=F32)


def nn(a, b):
    return lax.dot_general(a, b, (((1,), (0,)), ((), ())), preferred_element_type=F32)


def rows(start, size):
    return pl.ds(pl.multiple_of(start, size), size)


def gather_rows(meta, pieces, out):
    m = meta[7]
    for f in range(FR):
        for flip, piece in enumerate(pieces):
            out[f, rows((m ^ flip) * OWN, OWN), :] = piece[f]


def conv_into(meta, weight, maps, wide, prod, finish):
    for lag in range(3):
        wide[:, lag * CH:(lag + 1) * CH] = weight[9 * lag:9 * lag + 9].reshape(9 * OWN, CH)
    for f in range(FR):
        seen = jnp.concatenate([maps[source(meta, f, lag)] for lag in range(3)], axis=0)
        prod[f] = nn(wide[...], seen)
        total = jnp.zeros((OWN, PIX), F32)
        for i, (u, v) in enumerate(STEPS):
            total = total + turn(prod[f, i * OWN:(i + 1) * OWN, :], -(SIDE * u + v)) * inside(u, v)
        finish(f, total)


def first_conv(meta, f0, f1, f2, f3, weight, slope, hidden, ordered, maps, wide, prod):
    gather_rows(meta, (f0, f1, f2, f3), maps)

    def finish(f, total):
        sigma = 1.0 / (1.0 + jnp.exp(-total))
        slope[f] = sigma * (1.0 + total * (1.0 - sigma))
        hidden[f] = (total * sigma).astype(BF16)
    conv_into(meta, weight, maps, wide, prod, finish)
    for f in range(FR):
        ordered[f] = arrange(meta, maps[f], "x")


def arrange(meta, value, axis):
    r = lax.broadcasted_iota(jnp.int32, (CH, CH), 0)
    c = lax.broadcasted_iota(jnp.int32, (CH, CH), 1)
    high, low, a, b = (4, 16, 6, 5) if axis == "x" else (16, 4, 5, 6)
    want = ((meta[4] + (r >> 2)) & 3) * 64 + ((meta[a] + (r >> 6)) & 3) * high
    want = want + ((meta[b] + (r >> 4)) & 3) * low + (r & 3)
    return nn(jnp.where(c == want, 1.0, 0.0).astype(BF16), value).astype(BF16)


def second_conv(meta, h0, h1, h2, h3, weight, frames, out, maps, wide, prod):
    gather_rows(meta, (h0, h1, h2, h3), maps)

    def finish(f, total):
        out[f] = (frames[f].astype(F32) + total).astype(BF16)
    conv_into(meta, weight, maps, wide, prod, finish)


def cut_grad(meta, ordered, taps, outs):
    lhs = jnp.concatenate([
        jnp.concatenate([ordered[source(meta, f, lag)] for f in range(FR)], axis=1) for lag in range(3)
    ], axis=0)
    both = nt(lhs, taps[...])
    for r, out in enumerate(outs):
        part = [both[lag * CH + 64 * r:lag * CH + 64 * r + 64] for lag in range(3)]
        for lag in range(3):
            out[:, 512 * lag:512 * lag + 512] = part[lag][:, 0:512].astype(out.dtype)
        out[:, 1536:1664] = jnp.concatenate([part[0][:, 512:], part[1][:, 512:]], axis=1).astype(out.dtype)
        out[:, 1664:1792] = jnp.concatenate([part[2][:, 512:], jnp.zeros((64, 64), F32)], axis=1).astype(out.dtype)


def second_grad_part(meta, h0, h1, h2, h3, taps, s1, s2, s3, own, maps, ordered):
    gather_rows(meta, (h0, h1, h2, h3), maps)
    for f in range(FR):
        ordered[f] = arrange(meta, maps[f], "y")
    cut_grad(meta, ordered, taps, (own, s1, s2, s3))


def hidden_grad_part(meta, cot, c_core, weight, w_core, keep, send, taps, both, flipped, total):
    core, half = meta[7] & 1, meta[7] >> 1
    r = lax.broadcasted_iota(jnp.int32, (128, CH), 0)
    c = lax.broadcasted_iota(jnp.int32, (128, CH), 1)
    want = jnp.where(r < OWN, half, 1 - half) * 128 + core * OWN + (r & 63)
    pick = jnp.where(c == want, 1.0, 0.0).astype(BF16)
    for who, ref in enumerate((weight, w_core)):
        for lag in range(3):
            w = ref[9 * lag:9 * lag + 9].reshape(9 * OWN, CH)
            flipped[lag * 128:(lag + 1) * 128, who * 576:(who + 1) * 576] = nt(pick, w).astype(BF16)
    total[...] = jnp.zeros(total.shape, F32)
    for f in range(FR):
        live = jnp.where(meta[f] >= 0, 1.0, 0.0)
        for who, ref in enumerate((cot, c_core)):
            g = ref[f].astype(F32) * live
            for i, (u, v) in enumerate(STEPS):
                at = (who * 9 + i) * OWN
                both[at:at + OWN, :] = turn(g * inside(u, v), SIDE * u + v).astype(BF16)
        taps[:, f * PIX:(f + 1) * PIX] = both[0:9 * OWN, :]
        terms = nn(flipped[...], both[...])
        for lag in range(3):
            at = source(meta, f, lag)
            total[at] = total[at] + terms[lag * 128:(lag + 1) * 128]
    keep[...] = total[:, 0:OWN, :]
    send[...] = total[:, OWN:128, :]


def first_grad_part(meta, slope, ha, hb, ordered, s1, s2, s3, own, taps):
    for f in range(FR):
        g = ((ha[f] + hb[f]) * slope[f]).astype(BF16).astype(F32)
        for i, (u, v) in enumerate(STEPS):
            taps[i * OWN:(i + 1) * OWN, f * PIX:(f + 1) * PIX] = turn(g * inside(u, v), SIDE * u + v).astype(BF16)
    cut_grad(meta, ordered, taps, (own, s1, s2, s3))


def cut_again(meta, own, r1, r2, r3, s1, s2, s3, keep):
    for k, out in enumerate((keep, s1, s2, s3)):
        part = slice(16 * k, 16 * k + 16)
        value = own[part, :] + r1[part, :].astype(F32) + r2[part, :].astype(F32) + r3[part, :].astype(F32)
        out[...] = value.astype(out.dtype)


def pack_z(meta, own1, a1, a2, a3, own2, b1, b2, b3, keep, s1, s2, s3):
    for g, (own, r1, r2, r3) in enumerate(((own1, a1, a2, a3), (own2, b1, b2, b3))):
        total = own[...] + r1[...].astype(F32) + r2[...].astype(F32) + r3[...].astype(F32)
        for k, out in enumerate((keep, s1, s2, s3)):
            for j in range(14):
                out[56 * g + 4 * j:56 * g + 4 * j + 4, :] = total[4 * k:4 * k + 4, 128 * j:128 * j + 128]


def add_z(meta, own, a1, a2, a3, first, second):
    for g, out in enumerate((first, second)):
        for t in range(TAPS):
            lag, step = t // 9, t % 9
            block, side = (4 * lag + step // 2, step % 2) if step < 8 else (12 + lag // 2, lag % 2)
            part, lane = slice(56 * g + 4 * block, 56 * g + 4 * block + 4), slice(64 * side, 64 * side + 64)
            out[t] = own[part, lane] + a1[part, lane] + a2[part, lane] + a3[part, lane]


def ring(value, axis):
    moves = {
        "x": lambda k: lambda z, y, x: (z, y, (x + k) % 4),
        "y": lambda k: lambda z, y, x: (z, (y + k) % 4, x),
        "z": lambda k: lambda z, y, x: ((z + k) % 4, y, x),
    }
    values = value if isinstance(value, (list, tuple)) else [value] * 3
    return [lax.ppermute(v, "dp", dp_perm(moves[axis](k))) for k, v in zip((1, 2, 3), values)]


def behind(value, other):
    return lax.optimization_barrier((value, other))[0]


def local(frames, frame_offsets, first_weight, second_weight, cotangent):
    d, m = lax.axis_index("dp"), lax.axis_index("mp")
    zl, y, x = d // 16, (d // 4) % 4, d % 4
    meta = jnp.concatenate([frame_offsets, jnp.stack([zl, y, x, m]).astype(jnp.int32)])

    big = 2 * TAPS * OWN * CH * FR * PIX
    one = shape((FR, OWN, PIX), F32)
    f_z = lax.ppermute(frames, "mp", mp_perm(2))
    f_c = lax.ppermute(frames, "mp", mp_perm(1))
    c_c = lax.ppermute(cotangent, "mp", mp_perm(1))
    w_c = lax.ppermute(second_weight, "mp", mp_perm(1))
    g_keep, g_send, taps = call(
        hidden_grad_part,
        (one, one, shape((9 * OWN, FR * PIX), BF16)),
        [pltpu.VMEM((18 * OWN, PIX), BF16), pltpu.VMEM((3 * 128, 18 * OWN), BF16), pltpu.VMEM((FR, 128, PIX), F32)],
        (meta, cotangent, c_c, second_weight, w_c), big,
    )
    g_got = lax.ppermute(behind(g_send, f_z), "mp", mp_perm(2))
    f_d = lax.ppermute(f_z, "mp", mp_perm(1))

    prod = pltpu.VMEM((FR, 9 * OWN, PIX), F32)
    wide = pltpu.VMEM((9 * OWN, 3 * CH), BF16)
    maps = pltpu.VMEM((FR, CH, PIX), BF16)
    slope, hidden, ordered = call(
        first_conv,
        (one, shape((FR, OWN, PIX), BF16), shape((FR, CH, PIX), BF16)),
        [maps, wide, prod], (meta, frames, f_c, f_z, f_d, first_weight), big, after=(g_send,),
    )
    h_z = lax.ppermute(hidden, "mp", mp_perm(2))
    h_c = lax.ppermute(hidden, "mp", mp_perm(1))

    sent, held = (shape((64, LANES), BF16),) * 3, shape((64, LANES), F32)
    *sends1, own1 = call(
        first_grad_part, (*sent, held), [pltpu.VMEM((9 * OWN, FR * PIX), BF16)],
        (meta, slope, g_keep, g_got, ordered), big,
    )
    got1 = ring(sends1, "x")

    h_d = lax.ppermute(h_z, "mp", mp_perm(1))
    *sends2, own2 = call(
        second_grad_part, (*sent, held), [maps, maps], (meta, hidden, h_c, h_z, h_d, taps), big, after=(own1,),
    )
    got2 = ring(sends2, "y")

    sent, held = (shape((16, LANES), BF16),) * 3, shape((16, LANES), F32)
    output = call(
        second_conv,
        shape((FR, OWN, PIX), BF16),
        [maps, wide, prod], (meta, hidden, h_c, h_z, h_d, second_weight, frames), big, after=(own2,),
    )
    *sends1, own1 = call(cut_again, (*sent, held), [], (meta, own1, *got1), after=(output,))
    got1 = ring(sends1, "y")
    *sends2, own2 = call(cut_again, (*sent, held), [], (meta, own2, *got2), after=(own1,))
    got2 = ring(sends2, "x")

    sum_z = shape((112, 128), F32)
    own, *sends = call(pack_z, (sum_z,) * 4, [], (meta, own1, *got1, own2, *got2))
    got = ring(sends, "z")
    first, second = call(add_z, (shape((TAPS, 4, OWN), F32),) * 2, [], (meta, own, *got))
    first, second = first.transpose(0, 2, 1), second.transpose(0, 2, 1)
    return output, first, second


def solution(mesh):
    in_specs = (
        P("dp", "mp", None),
        P("dp"),
        P(None, "mp", None),
        P(None, "mp", None),
        P("dp", "mp", None),
    )
    out_specs = (P("dp", "mp", None), P(None, "mp", "dp"), P(None, "mp", "dp"))
    return jax.shard_map(local, mesh=mesh, in_specs=in_specs, out_specs=out_specs, check_vma=False)
```

```python
import jax
import jax.numpy as jnp
from jax import lax
from jax.experimental import pallas as pl
from jax.experimental.pallas import tpu as pltpu
from jax.sharding import PartitionSpec as P

F32, BF16 = jnp.float32, jnp.bfloat16
SIDE, PIX, FR, CH, OWN, TAPS = 16, 256, 4, 256, 64, 27
STEPS = tuple((u, v) for u in (-1, 0, 1) for v in (-1, 0, 1))
LANES = 1792


def place(zl, y, x):
    return (zl * 4 + y) * 4 + x


def dp_perm(move):
    return [
        (place(z, y, x), place(*move(z, y, x)))
        for z in range(4) for y in range(4) for x in range(4)
    ]


def mp_perm(flip):
    return [(m, m ^ flip) for m in range(4)]


def call(kernel, outs, scratch, args, flops=0, after=()):
    specs = [pl.BlockSpec(memory_space=pltpu.SMEM)]
    specs += [pl.BlockSpec(memory_space=pltpu.VMEM)] * (len(args) - 1)
    specs += [pl.BlockSpec(memory_space=pl.ANY)] * len(after)
    size = sum(a.size * a.dtype.itemsize for a in args)
    n = len(args)

    def body(*refs):
        kernel(*refs[:n], *refs[n + len(after):])

    return pl.pallas_call(
        body,
        out_shape=outs,
        in_specs=specs,
        out_specs=jax.tree.map(lambda _: pl.BlockSpec(memory_space=pltpu.VMEM), outs),
        scratch_shapes=scratch,
        cost_estimate=pl.CostEstimate(flops=flops, bytes_accessed=size, transcendentals=0),
        compiler_params=pltpu.CompilerParams(vmem_limit_bytes=48 * 2**20),
    )(*args, *after)


def shape(dims, kind):
    return jax.ShapeDtypeStruct(dims, kind)


def inside(u, v):
    pos = lax.broadcasted_iota(jnp.int32, (1, PIX), 1)
    row, col = pos >> 4, pos & 15
    ok = (row + u >= 0) & (row + u < SIDE) & (col + v >= 0) & (col + v < SIDE)
    return jnp.where(ok, 1.0, 0.0).astype(F32)


def turn(value, step):
    return value if step % PIX == 0 else pltpu.roll(value, step % PIX, 1)


def source(meta, f, lag):
    return f - jnp.minimum(jnp.maximum(meta[f], 0), lag)


def nt(a, b):
    return lax.dot_general(a, b, (((1,), (1,)), ((), ())), preferred_element_type=F32)


def nn(a, b):
    return lax.dot_general(a, b, (((1,), (0,)), ((), ())), preferred_element_type=F32)


def rows(start, size):
    return pl.ds(pl.multiple_of(start, size), size)


def gather_rows(meta, pieces, out):
    m = meta[7]
    for f in range(FR):
        for flip, piece in enumerate(pieces):
            out[f, rows((m ^ flip) * OWN, OWN), :] = piece[f]


def conv_into(meta, weight, maps, wide, prod, finish):
    for lag in range(3):
        wide[:, lag * CH:(lag + 1) * CH] = weight[9 * lag:9 * lag + 9].reshape(9 * OWN, CH)
    for f in range(FR):
        seen = jnp.concatenate([maps[source(meta, f, lag)] for lag in range(3)], axis=0)
        prod[f] = nn(wide[...], seen)
        total = jnp.zeros((OWN, PIX), F32)
        for i, (u, v) in enumerate(STEPS):
            total = total + turn(prod[f, i * OWN:(i + 1) * OWN, :], -(SIDE * u + v)) * inside(u, v)
        finish(f, total)


def first_conv(meta, f0, f1, f2, f3, weight, slope, hidden, ordered, maps, wide, prod):
    gather_rows(meta, (f0, f1, f2, f3), maps)

    def finish(f, total):
        sigma = 1.0 / (1.0 + jnp.exp(-total))
        slope[f] = sigma * (1.0 + total * (1.0 - sigma))
        hidden[f] = (total * sigma).astype(BF16)
    conv_into(meta, weight, maps, wide, prod, finish)
    for f in range(FR):
        ordered[f] = arrange(meta, maps[f], "x")


def arrange(meta, value, axis):
    r = lax.broadcasted_iota(jnp.int32, (CH, CH), 0)
    c = lax.broadcasted_iota(jnp.int32, (CH, CH), 1)
    high, low, a, b = (4, 16, 6, 5) if axis == "x" else (16, 4, 5, 6)
    want = ((meta[4] + (r >> 2)) & 3) * 64 + ((meta[a] + (r >> 6)) & 3) * high
    want = want + ((meta[b] + (r >> 4)) & 3) * low + (r & 3)
    return nn(jnp.where(c == want, 1.0, 0.0).astype(BF16), value).astype(BF16)


def second_conv(meta, h0, h1, h2, h3, weight, frames, out, maps, wide, prod):
    gather_rows(meta, (h0, h1, h2, h3), maps)

    def finish(f, total):
        out[f] = (frames[f].astype(F32) + total).astype(BF16)
    conv_into(meta, weight, maps, wide, prod, finish)


def cut_grad(meta, ordered, taps, outs):
    lhs = jnp.concatenate([
        jnp.concatenate([ordered[source(meta, f, lag)] for f in range(FR)], axis=1) for lag in range(3)
    ], axis=0)
    both = nt(lhs, taps[...])
    for r, out in enumerate(outs):
        part = [both[lag * CH + 64 * r:lag * CH + 64 * r + 64] for lag in range(3)]
        for lag in range(3):
            out[:, 512 * lag:512 * lag + 512] = part[lag][:, 0:512].astype(out.dtype)
        out[:, 1536:1664] = jnp.concatenate([part[0][:, 512:], part[1][:, 512:]], axis=1).astype(out.dtype)
        out[:, 1664:1792] = jnp.concatenate([part[2][:, 512:], jnp.zeros((64, 64), F32)], axis=1).astype(out.dtype)


def second_grad_part(meta, h0, h1, h2, h3, taps, s1, s2, s3, own, maps, ordered):
    gather_rows(meta, (h0, h1, h2, h3), maps)
    for f in range(FR):
        ordered[f] = arrange(meta, maps[f], "y")
    cut_grad(meta, ordered, taps, (own, s1, s2, s3))


def hidden_grad_part(meta, cot, c_core, weight, w_core, keep, send, taps, both, flipped, total):
    core, half = meta[7] & 1, meta[7] >> 1
    r = lax.broadcasted_iota(jnp.int32, (128, CH), 0)
    c = lax.broadcasted_iota(jnp.int32, (128, CH), 1)
    want = jnp.where(r < OWN, half, 1 - half) * 128 + core * OWN + (r & 63)
    pick = jnp.where(c == want, 1.0, 0.0).astype(BF16)
    for who, ref in enumerate((weight, w_core)):
        for lag in range(3):
            w = ref[9 * lag:9 * lag + 9].reshape(9 * OWN, CH)
            flipped[lag * 128:(lag + 1) * 128, who * 576:(who + 1) * 576] = nt(pick, w).astype(BF16)
    total[...] = jnp.zeros(total.shape, F32)
    for f in range(FR):
        live = jnp.where(meta[f] >= 0, 1.0, 0.0)
        for who, ref in enumerate((cot, c_core)):
            g = ref[f].astype(F32) * live
            for i, (u, v) in enumerate(STEPS):
                at = (who * 9 + i) * OWN
                both[at:at + OWN, :] = turn(g * inside(u, v), SIDE * u + v).astype(BF16)
        taps[:, f * PIX:(f + 1) * PIX] = both[0:9 * OWN, :]
        terms = nn(flipped[...], both[...])
        for lag in range(3):
            at = source(meta, f, lag)
            total[at] = total[at] + terms[lag * 128:(lag + 1) * 128]
    keep[...] = total[:, 0:OWN, :]
    send[...] = total[:, OWN:128, :]


def first_grad_part(meta, slope, ha, hb, ordered, s1, s2, s3, own, taps):
    for f in range(FR):
        g = ((ha[f] + hb[f]) * slope[f]).astype(BF16).astype(F32)
        for i, (u, v) in enumerate(STEPS):
            taps[i * OWN:(i + 1) * OWN, f * PIX:(f + 1) * PIX] = turn(g * inside(u, v), SIDE * u + v).astype(BF16)
    cut_grad(meta, ordered, taps, (own, s1, s2, s3))


def cut_again(meta, own, r1, r2, r3, s1, s2, s3, keep):
    for k, out in enumerate((keep, s1, s2, s3)):
        part = slice(16 * k, 16 * k + 16)
        value = own[part, :] + r1[part, :].astype(F32) + r2[part, :].astype(F32) + r3[part, :].astype(F32)
        out[...] = value.astype(out.dtype)


def pack_z(meta, own1, a1, a2, a3, own2, b1, b2, b3, keep, s1, s2, s3, rows_of):
    for g, (own, r1, r2, r3) in enumerate(((own1, a1, a2, a3), (own2, b1, b2, b3))):
        total = own[...] + r1[...].astype(F32) + r2[...].astype(F32) + r3[...].astype(F32)
        for k in range(4):
            for j in range(14):
                rows_of[k, 56 * g + 4 * j:56 * g + 4 * j + 4, :] = total[4 * k:4 * k + 4, 128 * j:128 * j + 128]
    for k, out in enumerate((keep, s1, s2, s3)):
        out[...] = rows_of[k].astype(out.dtype)


def add_z(meta, own, a1, a2, a3, first, second, total):
    total[...] = own[...] + a1[...].astype(F32) + a2[...].astype(F32) + a3[...].astype(F32)
    for g, out in enumerate((first, second)):
        for t in range(TAPS):
            lag, step = t // 9, t % 9
            block, side = (4 * lag + step // 2, step % 2) if step < 8 else (12 + lag // 2, lag % 2)
            part, lane = slice(56 * g + 4 * block, 56 * g + 4 * block + 4), slice(64 * side, 64 * side + 64)
            out[t] = total[part, lane]


def ring(value, axis):
    moves = {
        "x": lambda k: lambda z, y, x: (z, y, (x + k) % 4),
        "y": lambda k: lambda z, y, x: (z, (y + k) % 4, x),
        "z": lambda k: lambda z, y, x: ((z + k) % 4, y, x),
    }
    values = value if isinstance(value, (list, tuple)) else [value] * 3
    return [lax.ppermute(v, "dp", dp_perm(moves[axis](k))) for k, v in zip((1, 2, 3), values)]


def behind(value, other):
    return lax.optimization_barrier((value, other))[0]


def local(frames, frame_offsets, first_weight, second_weight, cotangent):
    d, m = lax.axis_index("dp"), lax.axis_index("mp")
    zl, y, x = d // 16, (d // 4) % 4, d % 4
    meta = jnp.concatenate([frame_offsets, jnp.stack([zl, y, x, m]).astype(jnp.int32)])

    big = 2 * TAPS * OWN * CH * FR * PIX
    one = shape((FR, OWN, PIX), F32)
    f_z = lax.ppermute(frames, "mp", mp_perm(2))
    f_c = lax.ppermute(frames, "mp", mp_perm(1))
    c_c = lax.ppermute(cotangent, "mp", mp_perm(1))
    w_c = lax.ppermute(second_weight, "mp", mp_perm(1))
    g_keep, g_send, taps = call(
        hidden_grad_part,
        (one, one, shape((9 * OWN, FR * PIX), BF16)),
        [pltpu.VMEM((18 * OWN, PIX), BF16), pltpu.VMEM((3 * 128, 18 * OWN), BF16), pltpu.VMEM((FR, 128, PIX), F32)],
        (meta, cotangent, c_c, second_weight, w_c), big,
    )
    g_got = lax.ppermute(behind(g_send, f_z), "mp", mp_perm(2))
    f_d = lax.ppermute(f_z, "mp", mp_perm(1))

    prod = pltpu.VMEM((FR, 9 * OWN, PIX), F32)
    wide = pltpu.VMEM((9 * OWN, 3 * CH), BF16)
    maps = pltpu.VMEM((FR, CH, PIX), BF16)
    slope, hidden, ordered = call(
        first_conv,
        (one, shape((FR, OWN, PIX), BF16), shape((FR, CH, PIX), BF16)),
        [maps, wide, prod], (meta, frames, f_c, f_z, f_d, first_weight), big, after=(g_send,),
    )
    h_z = lax.ppermute(hidden, "mp", mp_perm(2))
    h_c = lax.ppermute(hidden, "mp", mp_perm(1))

    sent, held = (shape((64, LANES), BF16),) * 3, shape((64, LANES), F32)
    *sends1, own1 = call(
        first_grad_part, (*sent, held), [pltpu.VMEM((9 * OWN, FR * PIX), BF16)],
        (meta, slope, g_keep, g_got, ordered), big,
    )
    got1 = ring(sends1, "x")

    h_d = lax.ppermute(h_z, "mp", mp_perm(1))
    *sends2, own2 = call(
        second_grad_part, (*sent, held), [maps, maps], (meta, hidden, h_c, h_z, h_d, taps), big, after=(own1,),
    )
    got2 = ring(sends2, "y")

    sent, held = (shape((16, LANES), BF16),) * 3, shape((16, LANES), F32)
    output = call(
        second_conv,
        shape((FR, OWN, PIX), BF16),
        [maps, wide, prod], (meta, hidden, h_c, h_z, h_d, second_weight, frames), big, after=(own2,),
    )
    *sends1, own1 = call(cut_again, (*sent, held), [], (meta, own1, *got1), after=(output,))
    got1 = ring(sends1, "y")
    *sends2, own2 = call(cut_again, (*sent, held), [], (meta, own2, *got2), after=(own1,))
    got2 = ring(sends2, "x")

    sum_z, sent = shape((112, 128), F32), shape((112, 128), BF16)
    own, *sends = call(
        pack_z, (sum_z, sent, sent, sent), [pltpu.VMEM((4, 112, 128), F32)], (meta, own1, *got1, own2, *got2),
    )
    got = ring(sends, "z")
    first, second = call(
        add_z, (shape((TAPS, 4, OWN), F32),) * 2, [pltpu.VMEM((112, 128), F32)], (meta, own, *got),
    )
    first, second = first.transpose(0, 2, 1), second.transpose(0, 2, 1)
    return output, first, second


def solution(mesh):
    in_specs = (
        P("dp", "mp", None),
        P("dp"),
        P(None, "mp", None),
        P(None, "mp", None),
        P("dp", "mp", None),
    )
    out_specs = (P("dp", "mp", None), P(None, "mp", "dp"), P(None, "mp", "dp"))
    return jax.shard_map(local, mesh=mesh, in_specs=in_specs, out_specs=out_specs, check_vma=False)
```
